32 devices in a mesh: segment: 4 (over z), exp: 8 (over y, x, core).
Axes of the slice: x: 2, y: 2, z: 4, core: 2. Of those that a mesh axis runs over, the one named last changes fastest.
Arguments:
- hidden_rows: bfloat16 [4096, 2048], P(('segment', 'exp')), may hold values from -60 to 60, as said below
- norm_gain: float32 [2048], replicated, may hold values from 0.5 to 1.5
- router_weight: bfloat16 [2048, 16], replicated, may hold values from -0.25 to 0.25
- expert_ids: int32 [4096, 6], P(('segment', 'exp')), may hold values from 0 to 15, all different within a row; in each aligned block of 64 rows (0 to 63, 64 to 127, ...) at most 30 rows name the same one
- gate_weight: bfloat16 [4, 8, 704, 2048], P('segment', 'exp'), may hold values from -0.125 to 0.125
- up_weight: bfloat16 [4, 8, 704, 2048], P('segment', 'exp'), may hold values from -0.125 to 0.125
- down_weight: bfloat16 [4, 8, 704, 2048], P('segment', 'exp'), may hold values from -0.15625 to 0.15625
- latent_gain: float32 [2048], replicated, may hold values from 0.5 to 1.5
- kv_weight: bfloat16 [2048, 512], replicated, may hold values from -0.125 to 0.125
Outputs:
- expert_mix: bfloat16 [4096, 2048], P(('segment', 'exp'))
- latents: bfloat16 [4096, 512], P(('segment', 'exp'))
- gram_input: float32 [4, 8, 1024, 2048], P('segment', 'exp')
- gram_hidden: float32 [4, 8, 704, 1408], P('segment', 'exp')
The draws below stay inside these ranges and needn't reach their ends.
Inputs may be any that keep to these rules, and one draw needn't show every extreme that they name: `expert_ids`: each row names 6 different experts and every expert is named somewhere. In each aligned block of 64 rows (one micro-batch of one device) no expert is named more than 30 times, and in some blocks some expert is named exactly 30 times. `hidden_rows`: activations of the attention section.
All inputs are finite; a program needn't handle non-finite values.
Results may differ from the reference program's by a relative error of at most 0.0068.
Values may be sent and summed in bfloat16 or wider, within the bound.
A program may use at most 192 MiB of HBM per device.

```python
import math
import jax
import jax.numpy as jnp
import numpy as np
from jax import lax

D = 2048
FF = 1408
KV_RANK = 512
TOPK = 6
MB_TOK = 64
TOKENS = 4096
PAIRS = 2
EXPERTS = 16
HALF = 704
CAP = 30
N_SEGMENT = 4
N_EXP = 8


def draw_hidden_rows(key, part):
    key_base, key_rows, key_cols = jax.random.split(key, 3)
    row_scale = jnp.exp(jax.random.uniform(key_rows, (TOKENS, 1), jnp.float32, math.log(0.3), math.log(3.0)))
    col_scale = jnp.exp(jax.random.uniform(key_cols, (1, D), jnp.float32, math.log(0.4), math.log(4.0)))
    values = jnp.clip(jax.random.normal(key_base, (TOKENS, D), jnp.float32), -5.0, 5.0)
    return (values * row_scale * col_scale).astype(jnp.bfloat16)


def steps_of(own_key, shape, cuts, low, high):
    def one(axis_at, blocks):
        draws = jax.random.uniform(jax.random.fold_in(jax.random.fold_in(own_key, 6), axis_at), (blocks,), jnp.float32, low / len(cuts), high / len(cuts))
        return jnp.repeat(jnp.exp(draws), shape[axis_at] // blocks).reshape((-1,) + (1,) * (len(shape) - axis_at - 1))

    factor_of = one(*cuts[0])
    for cut in cuts[1:]:
        factor_of = factor_of * one(*cut)
    return factor_of


def shared_out(own_key, own, number, rows, number_of, top, limit, lean):
    ranking = jax.random.permutation(own_key, number_of)
    crowded, common = load_shares(number_of, rows * top, limit, lean, True), load_shares(number_of, rows * top, limit, lean, False)
    places = jnp.arange(number_of)

    def named(sizes, offset_by):
        used = int((sizes > 0).sum())
        fixed = max(1, used // 4)
        passed = fixed + (places - fixed + offset_by * (used - fixed)) % max(1, number_of - fixed)
        return jnp.zeros((number_of,), jnp.int32).at[ranking[jnp.where(places < fixed, places, passed)]].set(jnp.asarray(sizes, jnp.int32))

    sizes = jnp.where(number % 4 == 0, named(crowded, number // 4), named(common, number - number // 4 - 1))
    mixed = jax.random.permutation(jax.random.fold_in(own, 3), number_of)
    donor, sink = mixed[0:number_of // 2 * 2:2], mixed[1:number_of // 2 * 2:2]
    margin = jnp.minimum(sizes[donor] - 1, limit - sizes[sink]) // 2
    margin = jnp.where((donor == ranking[0]) | (sink == ranking[0]) | (sizes[sink] == 0), 0, jnp.maximum(margin, 0))
    passed = jax.random.randint(jax.random.fold_in(own, 4), (number_of // 2,), 0, 1 << 20) % (margin + 1)
    sizes = sizes.at[donor].add(-passed).at[sink].add(passed)
    members = jnp.searchsorted(jnp.cumsum(sizes), jnp.arange(rows * top), side="right").astype(jnp.int32)
    table = members.reshape(top, rows).T
    table = table[jax.random.permutation(jax.random.fold_in(own, 1), rows)]
    offset_by = jax.random.randint(jax.random.fold_in(own, 2), (rows, 1), 0, top)
    return jnp.take_along_axis(table, (jnp.arange(top)[None, :] + offset_by) % top, axis=1)


def load_shares(number_of, total, reach, slope, full):
    loads = [(1 << 20) // math.isqrt(rank ** slope) + 1 for rank in range(1, number_of + 1)]
    largest = reach if full else min(reach, max(-(-total // number_of), total * loads[0] // sum(loads)))
    least = 1 if total - largest >= number_of - 1 else 0
    given, spare = [largest] + [least] * (number_of - 1), total - largest - least * (number_of - 1)
    while spare > 0:
        candidates = [i for i in range(1, number_of) if given[i] < largest] or [i for i in range(1, number_of) if given[i] < reach]
        whole, budget = sum([loads[i] for i in candidates]), spare
        for i in candidates:
            more = min(reach - given[i], max(1, budget * loads[i] // whole), spare)
            given[i] = given[i] + more
            spare = spare - more
    return np.array(given)


def scatter_about(stream_key, dims, deviation, reach, cuts=(), kind=jnp.bfloat16):
    factor_of = steps_of(stream_key, dims, cuts, -0.22, 0.18) if cuts else 1.0
    drawn = jax.random.normal(stream_key, dims, jnp.float32) * deviation * factor_of
    return jnp.minimum(jnp.maximum(drawn, -reach), reach).astype(kind)


def setup_inputs(seed: int = 0) -> dict:
    arg_keys = jax.random.split(jax.random.key(seed), 10)
    hidden_rows = draw_hidden_rows(jax.random.fold_in(arg_keys[9], 71), 0)
    norm_gain = jnp.clip(1.0 + 0.1 * jax.random.normal(arg_keys[1], (D,), jnp.float32), 0.5, 1.5)
    router_weight = scatter_about(arg_keys[2], (D, EXPERTS), (D // 4) ** -0.5, 0.25)
    expert_ids_keys = jax.random.split(jax.random.fold_in(arg_keys[3], 1), TOKENS // MB_TOK)
    expert_ids_turns = jax.random.permutation(jax.random.fold_in(arg_keys[3], 3), TOKENS // MB_TOK)
    expert_ids = jax.vmap(lambda own, number: shared_out(jax.random.fold_in(arg_keys[3], 2), own, number, MB_TOK, EXPERTS, TOPK, CAP, 1))(expert_ids_keys, expert_ids_turns).reshape((TOKENS, TOPK))
    gate_weight = scatter_about(arg_keys[4], (N_SEGMENT, N_EXP, HALF, D), D ** -0.5, 0.125, ((0, 4), (1, 8)))
    up_weight = scatter_about(arg_keys[5], (N_SEGMENT, N_EXP, HALF, D), D ** -0.5, 0.125, ((0, 4), (1, 8)))
    down_weight = scatter_about(arg_keys[6], (N_SEGMENT, N_EXP, HALF, D), FF ** -0.5, 0.15625, ((0, 4), (1, 8)))
    latent_gain = jnp.clip(1.0 + 0.1 * jax.random.normal(arg_keys[7], (D,), jnp.float32), 0.5, 1.5)
    kv_weight = scatter_about(arg_keys[8], (D, KV_RANK), D ** -0.5, 0.125)
    return dict(hidden_rows=hidden_rows, norm_gain=norm_gain, router_weight=router_weight, expert_ids=expert_ids, gate_weight=gate_weight, up_weight=up_weight, down_weight=down_weight, latent_gain=latent_gain, kv_weight=kv_weight)


def rms_norm(values, gain):
    mean_square = lax.optimization_barrier(jnp.mean(values * values, axis=-1, keepdims=True))
    return values * lax.rsqrt(mean_square + 1e-06) * gain

def reference(hidden_rows, norm_gain, router_weight, expert_ids, gate_weight, up_weight, down_weight, latent_gain, kv_weight):
    residual = hidden_rows.astype(jnp.float32)
    normed = rms_norm(residual, norm_gain).astype(jnp.bfloat16)
    logits = jnp.dot(normed, router_weight, preferred_element_type=jnp.float32)
    picked = jnp.take_along_axis(logits, expert_ids, axis=1)
    affinity = jax.nn.sigmoid(picked)
    gate_share = affinity / lax.optimization_barrier(jnp.sum(affinity, axis=1, keepdims=True))
    blocks = TOKENS // MB_TOK
    flat_ids = expert_ids.reshape(blocks, MB_TOK * TOPK)
    onehot = (flat_ids[:, :, None] == jnp.arange(EXPERTS, dtype=jnp.int32)[None, None, :]).astype(jnp.int32)
    slot_rank = lax.optimization_barrier(jnp.sum((jnp.cumsum(onehot, axis=1) - onehot) * onehot, axis=2))
    counts = lax.optimization_barrier(jnp.sum(onehot, axis=(0, 1)))
    position = (jnp.arange(blocks, dtype=jnp.int32)[:, None] * CAP + slot_rank).reshape(TOKENS, TOPK)
    slot_total = blocks * CAP
    token_index = jnp.broadcast_to(jnp.arange(TOKENS, dtype=jnp.int32)[:, None], (TOKENS, TOPK))
    token_row = jnp.full((EXPERTS, slot_total), TOKENS, jnp.int32).at[expert_ids, position].set(token_index)
    gate_table = jnp.zeros((EXPERTS, slot_total), jnp.float32).at[expert_ids, position].set(gate_share)
    padded_rows = jnp.concatenate([normed, jnp.zeros((1, D), jnp.bfloat16)], axis=0)

    def expert_step(mix_rows, inputs):
        expert, rows_index, gate_row, count = inputs
        pair_index = expert // N_EXP
        column = expert % N_EXP
        gate_full = jnp.concatenate([gate_weight[2 * pair_index, column], gate_weight[2 * pair_index + 1, column]], axis=0)
        up_full = jnp.concatenate([up_weight[2 * pair_index, column], up_weight[2 * pair_index + 1, column]], axis=0)
        down_full = jnp.concatenate([down_weight[2 * pair_index, column], down_weight[2 * pair_index + 1, column]], axis=0)
        expert_rows = padded_rows[rows_index]
        gate_pre = jnp.dot(expert_rows, gate_full.T, preferred_element_type=jnp.float32)
        up_pre = jnp.dot(expert_rows, up_full.T, preferred_element_type=jnp.float32)
        hidden = (jax.nn.silu(gate_pre) * up_pre).astype(jnp.bfloat16)
        output_rows = jnp.dot(hidden, down_full, preferred_element_type=jnp.float32)
        mix_rows = mix_rows.at[rows_index].add(output_rows * gate_row[:, None])
        inverse_count = 2.0 / count.astype(jnp.float32)
        gram_in = jnp.dot(expert_rows.T, expert_rows, preferred_element_type=jnp.float32) * inverse_count
        gram_hid = jnp.dot(hidden.T, hidden, preferred_element_type=jnp.float32) * inverse_count
        return (mix_rows, (gram_in, gram_hid))
    start_mix = jnp.zeros((TOKENS + 1, D), jnp.float32)
    mix_rows, grams = lax.scan(expert_step, start_mix, (jnp.arange(EXPERTS, dtype=jnp.int32), token_row, gate_table, counts))
    expert_mix = mix_rows[:TOKENS].astype(jnp.bfloat16)
    combined = residual + expert_mix.astype(jnp.float32)
    normed_next = rms_norm(combined, latent_gain).astype(jnp.bfloat16)
    latents = jnp.dot(normed_next, kv_weight, preferred_element_type=jnp.float32).astype(jnp.bfloat16)
    gram_input = grams[0].reshape(PAIRS, N_EXP, 2, D // 2, D).transpose(0, 2, 1, 3, 4).reshape(N_SEGMENT, N_EXP, D // 2, D)
    gram_hidden = grams[1].reshape(PAIRS, N_EXP, 2, HALF, FF).transpose(0, 2, 1, 3, 4).reshape(N_SEGMENT, N_EXP, HALF, FF)
    return (expert_mix, latents, gram_input, gram_hidden)
```

```python
import jax
import jax.numpy as jnp
from jax import lax
from jax.sharding import PartitionSpec as P

MB_TOK = 64


def swapped(value, axis, stride):
    mask = 2**stride
    pairs = [(source, source ^ mask) for source in range(lax.axis_size(axis))]
    return lax.ppermute(value, axis, pairs)


def rms_norm(values, gain):
    mean_square = jnp.mean(values * values, axis=-1, keepdims=True)
    return values * lax.rsqrt(mean_square + 1e-06) * gain


def dispatch_body(
    hidden_rows,
    norm_gain,
    router_weight,
    expert_ids,
    gate_weight,
    up_weight,
    down_weight,
    latent_gain,
    kv_weight,
):
    segments = lax.axis_size("segment")
    columns = lax.axis_size("exp")
    devices = segments * columns
    pair_count = segments // 2
    model_width = hidden_rows.shape[1]
    width_half = model_width // 2
    experts = router_weight.shape[1]
    top_count = expert_ids.shape[1]
    tok_rows = hidden_rows.shape[0]
    micro_rows = MB_TOK
    capacity = micro_rows * top_count * 5 // (4 * experts)
    half_index = lax.axis_index("segment") % 2
    w_gate = gate_weight[0, 0]
    w_up = up_weight[0, 0]
    w_down = down_weight[0, 0]
    half_units = w_gate.shape[0]
    slot_rows = devices * capacity
    own_rows = lax.dynamic_slice_in_dim(w_down, half_index * width_half, width_half, 1)
    sent_rows = lax.dynamic_slice_in_dim(w_down, (1 - half_index) * width_half, width_half, 1)
    other_rows = swapped(sent_rows, "segment", 0)
    down_block = jnp.where(
        half_index == 0,
        jnp.concatenate([own_rows, other_rows], axis=0),
        jnp.concatenate([other_rows, own_rows], axis=0),
    )
    residual = hidden_rows.astype(jnp.float32)
    normed = rms_norm(residual, norm_gain).astype(jnp.bfloat16)
    logits = jnp.dot(normed, router_weight, preferred_element_type=jnp.float32)
    expert_grid = jnp.arange(experts, dtype=jnp.int32)
    choose = expert_ids[:, :, None] == expert_grid[None, None, :]
    picked = jnp.sum(jnp.where(choose, logits[:, None, :], 0.0), axis=2)
    affinity = jax.nn.sigmoid(picked)
    gate_share = affinity / jnp.sum(affinity, axis=1, keepdims=True)
    gram_in = jnp.zeros((width_half, model_width), jnp.float32)
    gram_hid = jnp.zeros((half_units, 2 * half_units), jnp.float32)
    count_total = jnp.zeros((), jnp.float32)
    mix_blocks = []
    positions = jnp.arange(experts * capacity, dtype=jnp.int32)
    pair_rows = jnp.arange(micro_rows * top_count, dtype=jnp.int32)
    earlier = (pair_rows[:, None] > pair_rows[None, :]).astype(jnp.bfloat16)
    for step_index in range(tok_rows // micro_rows):
        low = step_index * micro_rows
        block_rows = normed[low : low + micro_rows]
        block_ids = expert_ids[low : low + micro_rows]
        block_gates = gate_share[low : low + micro_rows]
        flat_ids = block_ids.reshape(-1)
        onehot = (flat_ids[:, None] == expert_grid[None, :]).astype(jnp.int32)
        before = jnp.dot(
            earlier, onehot.astype(jnp.bfloat16), preferred_element_type=jnp.float32
        ).astype(jnp.int32)
        slot_rank = jnp.sum(before * onehot, axis=1)
        target = (flat_ids * capacity + slot_rank).reshape(micro_rows, top_count)
        picker = target[:, :, None] == positions[None, None, :]
        dispatch_table = jnp.any(picker, axis=1).astype(jnp.bfloat16)
        combine_table = jnp.sum(jnp.where(picker, block_gates[:, :, None], 0.0), axis=1)
        buffer = lax.dot_general(
            dispatch_table, block_rows, (((0,), (0,)), ((), ())), preferred_element_type=jnp.float32
        ).astype(jnp.bfloat16)
        sent_counts = jnp.sum(onehot, axis=0).astype(jnp.bfloat16)
        grid_rows = jnp.broadcast_to(
            buffer.reshape(pair_count, 1, columns, capacity, model_width),
            (pair_count, 2, columns, capacity, model_width),
        ).reshape(devices, capacity, model_width)
        grid_counts = jnp.broadcast_to(
            sent_counts.reshape(pair_count, 1, columns), (pair_count, 2, columns)
        ).reshape(devices, 1)
        arrived, arrived_counts = (
            lax.all_to_all(grid_rows, ("segment", "exp"), split_axis=0, concat_axis=0, tiled=True),
            lax.all_to_all(
                grid_counts, ("segment", "exp"), split_axis=0, concat_axis=0, tiled=True
            ),
        )
        received = arrived.reshape(slot_rows, model_width)
        count_total = count_total + jnp.sum(arrived_counts.astype(jnp.float32))
        gate_pre = lax.dot_general(
            w_gate, received, (((1,), (1,)), ((), ())), preferred_element_type=jnp.float32
        )
        up_pre = lax.dot_general(
            w_up, received, (((1,), (1,)), ((), ())), preferred_element_type=jnp.float32
        )
        hidden_t = (jax.nn.silu(gate_pre) * up_pre).astype(jnp.bfloat16)
        own_columns = lax.dynamic_slice_in_dim(received, half_index * width_half, width_half, 1)
        gram_in = gram_in + lax.dot_general(
            own_columns, received, (((0,), (0,)), ((), ())), preferred_element_type=jnp.float32
        )
        other_hidden = swapped(hidden_t, "segment", 0)
        first_half = jnp.where(half_index == 0, hidden_t, other_hidden)
        second_half = jnp.where(half_index == 0, other_hidden, hidden_t)
        full_hidden = jnp.concatenate([first_half, second_half], axis=0)
        gram_hid = gram_hid + lax.dot_general(
            hidden_t, full_hidden, (((1,), (1,)), ((), ())), preferred_element_type=jnp.float32
        )
        column_half = lax.dot_general(
            full_hidden, down_block, (((0,), (0,)), ((), ())), preferred_element_type=jnp.float32
        )
        returned = lax.all_to_all(
            column_half.reshape(devices, capacity, width_half),
            ("segment", "exp"),
            split_axis=0,
            concat_axis=0,
            tiled=True,
        )
        expert_rows = (
            returned.reshape(pair_count, 2, columns, capacity, width_half)
            .transpose(0, 2, 3, 1, 4)
            .reshape(experts * capacity, model_width)
        )
        mix_rows = jnp.dot(
            combine_table,
            expert_rows,
            precision=lax.Precision.HIGHEST,
            preferred_element_type=jnp.float32,
        )
        mix_blocks.append(mix_rows)
    expert_mix = jnp.concatenate(mix_blocks, axis=0).astype(jnp.bfloat16)
    combined = residual + expert_mix.astype(jnp.float32)
    normed_next = rms_norm(combined, latent_gain).astype(jnp.bfloat16)
    latents = jnp.dot(normed_next, kv_weight, preferred_element_type=jnp.float32).astype(
        jnp.bfloat16
    )
    inverse_count = 2.0 / count_total
    gram_input = (gram_in * inverse_count)[None, None]
    gram_hidden = (gram_hid * inverse_count)[None, None]
    return (expert_mix, latents, gram_input, gram_hidden)


GROUP = 512


def exchanged(value, axis, mask):
    pairs = [(source, source ^ mask) for source in range(lax.axis_size(axis))]
    return lax.ppermute(value, axis, pairs)


def halve(value, dim, bit, axis, mask):
    kept = lax.dynamic_index_in_dim(value, bit, dim, keepdims=False)
    sent = lax.dynamic_index_in_dim(value, 1 - bit, dim, keepdims=False)
    came = exchanged(sent.astype(jnp.bfloat16), axis, mask)
    return kept.astype(jnp.float32) + came.astype(jnp.float32)


def gate_table(normed, router_weight, expert_ids):
    experts = router_weight.shape[1]
    logits = jnp.dot(normed, router_weight, preferred_element_type=jnp.float32)
    grid = jnp.arange(experts, dtype=jnp.int32)
    choose = jnp.any(expert_ids[:, :, None] == grid[None, None, :], axis=1)
    affinity = jnp.where(choose, jax.nn.sigmoid(logits), 0.0)
    share = affinity / jnp.sum(affinity, axis=1, keepdims=True)
    return jnp.where(choose, share, -1.0)


def gather_body(
    hidden_rows,
    norm_gain,
    router_weight,
    expert_ids,
    gate_weight,
    up_weight,
    down_weight,
    latent_gain,
    kv_weight,
):
    segment = lax.axis_index("segment")
    column = lax.axis_index("exp")
    columns = lax.axis_size("exp")
    half_index = segment % 2
    expert = (segment // 2) * columns + column
    core, along_x, along_y = column % 2, (column // 2) % 2, column // 4
    tok_rows, model_width = hidden_rows.shape
    width_half = model_width // 2
    experts = router_weight.shape[1]
    capacity = GROUP * expert_ids.shape[1] * 5 // (4 * experts)
    w_gate, w_up, w_down = gate_weight[0, 0], up_weight[0, 0], down_weight[0, 0]
    half_units = w_gate.shape[0]

    residual = hidden_rows.astype(jnp.float32)
    normed = rms_norm(residual, norm_gain).astype(jnp.bfloat16)
    table = gate_table(normed, router_weight, expert_ids)
    everywhere = ("segment", "exp")
    all_table = lax.all_gather(table, everywhere, axis=0, tiled=True)
    all_rows = lax.all_gather(normed, everywhere, axis=0, tiled=True)

    own = jnp.arange(experts, dtype=jnp.int32) == expert
    gates = jnp.sum(jnp.where(own[None, :], all_table, 0.0), axis=1).reshape(-1, GROUP)
    named = gates >= 0.0
    count = jnp.sum(named.astype(jnp.float32))
    place = jnp.arange(GROUP, dtype=jnp.int32)
    earlier = (place[:, None] < place[None, :]).astype(jnp.bfloat16)
    rank = jnp.dot(named.astype(jnp.bfloat16), earlier, preferred_element_type=jnp.float32)
    rank = jnp.where(named, rank.astype(jnp.int32), -1)
    slots = jnp.arange(capacity, dtype=jnp.int32)
    picks = rank[:, None, :] == slots[None, :, None]
    slot_gates = jnp.sum(jnp.where(picks, gates[:, None, :], 0.0), axis=2)
    picks = picks.astype(jnp.bfloat16)
    groups = picks.shape[0]

    rows = lax.dot_general(
        picks,
        all_rows.reshape(groups, GROUP, model_width),
        (((2,), (1,)), ((0,), (0,))),
        preferred_element_type=jnp.float32,
    ).astype(jnp.bfloat16)
    rows = rows.reshape(groups * capacity, model_width)
    by_units = (((1,), (1,)), ((), ()))
    gate_pre = lax.dot_general(rows, w_gate, by_units, preferred_element_type=jnp.float32)
    up_pre = lax.dot_general(rows, w_up, by_units, preferred_element_type=jnp.float32)
    hidden = (jax.nn.silu(gate_pre) * up_pre).astype(jnp.bfloat16)
    other_hidden = exchanged(hidden, "segment", 1)
    out = jnp.dot(hidden, w_down, preferred_element_type=jnp.float32)
    out = (out * slot_gates.reshape(-1, 1)).astype(jnp.bfloat16)
    mix = lax.dot_general(
        picks,
        out.reshape(groups, capacity, model_width),
        (((1,), (1,)), ((0,), (0,))),
        preferred_element_type=jnp.float32,
    ).astype(jnp.bfloat16)
    mix = mix.reshape(2, 2, 2, 2, 2, tok_rows, model_width)
    mix = halve(mix, 4, core, "exp", 1)
    first = halve(mix[..., :width_half], 3, along_x, "exp", 2)
    second = halve(mix[..., width_half:], 2, along_y, "exp", 4)
    first = halve(first, 2, along_y, "exp", 4)
    second = halve(second, 2, along_x, "exp", 2)
    mix = jnp.concatenate([first, second], axis=-1)
    mix = halve(mix, 0, segment // 2, "segment", 2)
    mix = halve(mix, 0, segment % 2, "segment", 1)

    expert_mix = mix.astype(jnp.bfloat16)
    combined = residual + expert_mix.astype(jnp.float32)
    normed_next = rms_norm(combined, latent_gain).astype(jnp.bfloat16)
    latents = jnp.dot(normed_next, kv_weight, preferred_element_type=jnp.float32).astype(
        jnp.bfloat16
    )
    by_slots = (((0,), (0,)), ((), ()))
    inverse_count = 2.0 / count
    own_columns = lax.dynamic_slice_in_dim(rows, half_index * width_half, width_half, 1)
    gram_in = lax.dot_general(own_columns, rows, by_slots, preferred_element_type=jnp.float32)
    first_half = jnp.where(half_index == 0, hidden, other_hidden)
    second_half = jnp.where(half_index == 0, other_hidden, hidden)
    full_hidden = jnp.concatenate([first_half, second_half], axis=1)
    gram_hid = lax.dot_general(hidden, full_hidden, by_slots, preferred_element_type=jnp.float32)
    return (
        expert_mix,
        latents,
        (gram_in * inverse_count)[None, None],
        (gram_hid * inverse_count)[None, None],
    )


def solution(mesh):
    return jax.shard_map(
        gather_body if mesh.shape["exp"] == 8 and mesh.shape["segment"] == 4 else dispatch_body,
        mesh=mesh,
        in_specs=(
            P(("segment", "exp"), None),
            P(),
            P(),
            P(("segment", "exp"), None),
            P("segment", "exp", None, None),
            P("segment", "exp", None, None),
            P("segment", "exp", None, None),
            P(),
            P(),
        ),
        out_specs=(
            P(("segment", "exp"), None),
            P(("segment", "exp"), None),
            P("segment", "exp", None, None),
            P("segment", "exp", None, None),
        ),
        check_vma=False,
    )
```

```python
import jax
import jax.numpy as jnp
from jax import lax
from jax.sharding import PartitionSpec as P

MB_TOK = 64


def swapped(value, axis, stride):
    mask = 2**stride
    pairs = [(source, source ^ mask) for source in range(lax.axis_size(axis))]
    return lax.ppermute(value, axis, pairs)


def rms_norm(values, gain):
    mean_square = jnp.mean(values * values, axis=-1, keepdims=True)
    return values * lax.rsqrt(mean_square + 1e-06) * gain


def dispatch_body(
    hidden_rows,
    norm_gain,
    router_weight,
    expert_ids,
    gate_weight,
    up_weight,
    down_weight,
    latent_gain,
    kv_weight,
):
    segments = lax.axis_size("segment")
    columns = lax.axis_size("exp")
    devices = segments * columns
    pair_count = segments // 2
    model_width = hidden_rows.shape[1]
    width_half = model_width // 2
    experts = router_weight.shape[1]
    top_count = expert_ids.shape[1]
    tok_rows = hidden_rows.shape[0]
    micro_rows = MB_TOK
    capacity = micro_rows * top_count * 5 // (4 * experts)
    half_index = lax.axis_index("segment") % 2
    w_gate = gate_weight[0, 0]
    w_up = up_weight[0, 0]
    w_down = down_weight[0, 0]
    half_units = w_gate.shape[0]
    slot_rows = devices * capacity
    own_rows = lax.dynamic_slice_in_dim(w_down, half_index * width_half, width_half, 1)
    sent_rows = lax.dynamic_slice_in_dim(w_down, (1 - half_index) * width_half, width_half, 1)
    other_rows = swapped(sent_rows, "segment", 0)
    down_block = jnp.where(
        half_index == 0,
        jnp.concatenate([own_rows, other_rows], axis=0),
        jnp.concatenate([other_rows, own_rows], axis=0),
    )
    residual = hidden_rows.astype(jnp.float32)
    normed = rms_norm(residual, norm_gain).astype(jnp.bfloat16)
    logits = jnp.dot(normed, router_weight, preferred_element_type=jnp.float32)
    expert_grid = jnp.arange(experts, dtype=jnp.int32)
    choose = expert_ids[:, :, None] == expert_grid[None, None, :]
    picked = jnp.sum(jnp.where(choose, logits[:, None, :], 0.0), axis=2)
    affinity = jax.nn.sigmoid(picked)
    gate_share = affinity / jnp.sum(affinity, axis=1, keepdims=True)
    gram_in = jnp.zeros((width_half, model_width), jnp.float32)
    gram_hid = jnp.zeros((half_units, 2 * half_units), jnp.float32)
    count_total = jnp.zeros((), jnp.float32)
    mix_blocks = []
    positions = jnp.arange(experts * capacity, dtype=jnp.int32)
    pair_rows = jnp.arange(micro_rows * top_count, dtype=jnp.int32)
    earlier = (pair_rows[:, None] > pair_rows[None, :]).astype(jnp.bfloat16)
    for step_index in range(tok_rows // micro_rows):
        low = step_index * micro_rows
        block_rows = normed[low : low + micro_rows]
        block_ids = expert_ids[low : low + micro_rows]
        block_gates = gate_share[low : low + micro_rows]
        flat_ids = block_ids.reshape(-1)
        onehot = (flat_ids[:, None] == expert_grid[None, :]).astype(jnp.int32)
        before = jnp.dot(
            earlier, onehot.astype(jnp.bfloat16), preferred_element_type=jnp.float32
        ).astype(jnp.int32)
        slot_rank = jnp.sum(before * onehot, axis=1)
        target = (flat_ids * capacity + slot_rank).reshape(micro_rows, top_count)
        picker = target[:, :, None] == positions[None, None, :]
        dispatch_table = jnp.any(picker, axis=1).astype(jnp.bfloat16)
        combine_table = jnp.sum(jnp.where(picker, block_gates[:, :, None], 0.0), axis=1)
        buffer = lax.dot_general(
            dispatch_table, block_rows, (((0,), (0,)), ((), ())), preferred_element_type=jnp.float32
        ).astype(jnp.bfloat16)
        sent_counts = jnp.sum(onehot, axis=0).astype(jnp.bfloat16)
        grid_rows = jnp.broadcast_to(
            buffer.reshape(pair_count, 1, columns, capacity, model_width),
            (pair_count, 2, columns, capacity, model_width),
        ).reshape(devices, capacity, model_width)
        grid_counts = jnp.broadcast_to(
            sent_counts.reshape(pair_count, 1, columns), (pair_count, 2, columns)
        ).reshape(devices, 1)
        arrived, arrived_counts = (
            lax.all_to_all(grid_rows, ("segment", "exp"), split_axis=0, concat_axis=0, tiled=True),
            lax.all_to_all(
                grid_counts, ("segment", "exp"), split_axis=0, concat_axis=0, tiled=True
            ),
        )
        received = arrived.reshape(slot_rows, model_width)
        count_total = count_total + jnp.sum(arrived_counts.astype(jnp.float32))
        gate_pre = lax.dot_general(
            w_gate, received, (((1,), (1,)), ((), ())), preferred_element_type=jnp.float32
        )
        up_pre = lax.dot_general(
            w_up, received, (((1,), (1,)), ((), ())), preferred_element_type=jnp.float32
        )
        hidden_t = (jax.nn.silu(gate_pre) * up_pre).astype(jnp.bfloat16)
        own_columns = lax.dynamic_slice_in_dim(received, half_index * width_half, width_half, 1)
        gram_in = gram_in + lax.dot_general(
            own_columns, received, (((0,), (0,)), ((), ())), preferred_element_type=jnp.float32
        )
        other_hidden = swapped(hidden_t, "segment", 0)
        first_half = jnp.where(half_index == 0, hidden_t, other_hidden)
        second_half = jnp.where(half_index == 0, other_hidden, hidden_t)
        full_hidden = jnp.concatenate([first_half, second_half], axis=0)
        gram_hid = gram_hid + lax.dot_general(
            hidden_t, full_hidden, (((1,), (1,)), ((), ())), preferred_element_type=jnp.float32
        )
        column_half = lax.dot_general(
            full_hidden, down_block, (((0,), (0,)), ((), ())), preferred_element_type=jnp.float32
        )
        returned = lax.all_to_all(
            column_half.reshape(devices, capacity, width_half),
            ("segment", "exp"),
            split_axis=0,
            concat_axis=0,
            tiled=True,
        )
        expert_rows = (
            returned.reshape(pair_count, 2, columns, capacity, width_half)
            .transpose(0, 2, 3, 1, 4)
            .reshape(experts * capacity, model_width)
        )
        mix_rows = jnp.dot(
            combine_table,
            expert_rows,
            precision=lax.Precision.HIGHEST,
            preferred_element_type=jnp.float32,
        )
        mix_blocks.append(mix_rows)
    expert_mix = jnp.concatenate(mix_blocks, axis=0).astype(jnp.bfloat16)
    combined = residual + expert_mix.astype(jnp.float32)
    normed_next = rms_norm(combined, latent_gain).astype(jnp.bfloat16)
    latents = jnp.dot(normed_next, kv_weight, preferred_element_type=jnp.float32).astype(
        jnp.bfloat16
    )
    inverse_count = 2.0 / count_total
    gram_input = (gram_in * inverse_count)[None, None]
    gram_hidden = (gram_hid * inverse_count)[None, None]
    return (expert_mix, latents, gram_input, gram_hidden)


GROUP = 512
CHUNKS = 2
PARTS = 3
LANES = 128


def exchanged(value, axis, mask):
    pairs = [(source, source ^ mask) for source in range(lax.axis_size(axis))]
    return lax.ppermute(value.astype(jnp.bfloat16), axis, pairs)


def gate_table(normed, router_weight, expert_ids):
    experts = router_weight.shape[1]
    logits = jnp.dot(normed, router_weight, preferred_element_type=jnp.float32)
    grid = jnp.arange(experts, dtype=jnp.int32)
    choose = jnp.any(expert_ids[:, :, None] == grid[None, None, :], axis=1)
    affinity = jnp.where(choose, jax.nn.sigmoid(logits), 0.0)
    share = affinity / jnp.sum(affinity, axis=1, keepdims=True)
    return jnp.where(choose, share, -1.0)


def in_parts(table):
    parts, rest = [], table
    for _ in range(PARTS):
        part = lax.reduce_precision(rest, 8, 7)
        parts.append(part.astype(jnp.bfloat16))
        rest = rest - part
    pad = LANES - PARTS * table.shape[1]
    return jnp.pad(jnp.concatenate(parts, axis=1), ((0, 0), (0, pad)))


def flipped_if(value, bit, dim):
    return jnp.where(bit == 1, jnp.flip(value, dim), value)


def gather_body(
    hidden_rows,
    norm_gain,
    router_weight,
    expert_ids,
    gate_weight,
    up_weight,
    down_weight,
    latent_gain,
    kv_weight,
):
    segment = lax.axis_index("segment")
    column = lax.axis_index("exp")
    columns = lax.axis_size("exp")
    segments = lax.axis_size("segment")
    half_index = segment % 2
    expert = (segment // 2) * columns + column
    core, along_x, along_y = column % 2, (column // 2) % 2, column // 4
    tok_rows, model_width = hidden_rows.shape
    width_half = model_width // 2
    experts = router_weight.shape[1]
    capacity = GROUP * expert_ids.shape[1] * 5 // (4 * experts)
    w_gate, w_up, w_down = gate_weight[0, 0], up_weight[0, 0], down_weight[0, 0]
    chunk_rows = tok_rows // CHUNKS
    tokens = segments * columns * chunk_rows
    groups = tokens // GROUP

    residual = hidden_rows.astype(jnp.float32)
    normed = rms_norm(residual, norm_gain).astype(jnp.bfloat16)
    table = in_parts(gate_table(normed, router_weight, expert_ids))
    packed = jnp.concatenate([normed, table], axis=1)
    gathered = [
        lax.all_gather(
            packed[chunk * chunk_rows : (chunk + 1) * chunk_rows],
            ("segment", "exp"),
            axis=0,
            tiled=True,
        )
        for chunk in range(CHUNKS)
    ]

    lane = jnp.arange(LANES, dtype=jnp.int32)
    own_lane = (lane % experts == expert) & (lane < PARTS * experts)
    place = jnp.arange(GROUP, dtype=jnp.int32)
    earlier = (place[:, None] < place[None, :]).astype(jnp.bfloat16)
    slots = jnp.arange(capacity, dtype=jnp.int32)
    by_units = (((1,), (1,)), ((), ()))
    by_slots = (((0,), (0,)), ((), ()))
    count = jnp.zeros((), jnp.float32)
    all_received, all_hidden, all_other, mixes = [], [], [], []
    for chunk in range(CHUNKS):
        if chunk:
            gathered[chunk], _ = lax.optimization_barrier((gathered[chunk], sent))
        tail = gathered[chunk][:, model_width:].astype(jnp.float32)
        gates = jnp.sum(jnp.where(own_lane[None, :], tail, 0.0), axis=1).reshape(groups, GROUP)
        named = gates >= 0.0
        count = count + jnp.sum(named.astype(jnp.float32))
        rank = jnp.dot(named.astype(jnp.bfloat16), earlier, preferred_element_type=jnp.float32)
        rank = jnp.where(named, rank.astype(jnp.int32), -1)
        picks = rank[:, None, :] == slots[None, :, None]
        slot_gates = jnp.sum(jnp.where(picks, gates[:, None, :], 0.0), axis=2)
        received = lax.dot_general(
            picks.astype(jnp.bfloat16),
            gathered[chunk][:, :model_width].reshape(groups, GROUP, model_width),
            (((2,), (1,)), ((0,), (0,))),
            preferred_element_type=jnp.float32,
        ).astype(jnp.bfloat16)
        received = received.reshape(groups * capacity, model_width)
        gate_pre = lax.dot_general(received, w_gate, by_units, preferred_element_type=jnp.float32)
        up_pre = lax.dot_general(received, w_up, by_units, preferred_element_type=jnp.float32)
        hidden = (jax.nn.silu(gate_pre) * up_pre).astype(jnp.bfloat16)
        all_received.append(received)
        all_hidden.append(hidden)
        all_other.append(exchanged(hidden, "segment", 1))
        out = jnp.dot(hidden, w_down, preferred_element_type=jnp.float32)
        out = (out * slot_gates.reshape(-1, 1)).astype(jnp.bfloat16)
        out = out.reshape(groups, capacity, model_width)

        near = rank.reshape(groups, 2, 2, 2, chunk_rows)
        near = flipped_if(flipped_if(flipped_if(near, core, 3), along_x, 2), along_y, 1)

        def scattered(places):
            hits = (places.reshape(groups, 1, -1) == slots[None, :, None]).astype(jnp.bfloat16)
            return lax.dot_general(
                hits, out, (((1,), (1,)), ((0,), (0,))), preferred_element_type=jnp.float32
            ).reshape(groups, 2, 2, chunk_rows, model_width)

        sent = scattered(near[:, :, :, 1]).astype(jnp.bfloat16)
        came = exchanged(sent, "exp", 1)
        mix = scattered(near[:, :, :, 0]) + came.astype(jnp.float32)
        first, second = mix[..., :width_half], mix[..., width_half:]
        first_came = exchanged(first[:, :, 1], "exp", 2)
        second_came = exchanged(second[:, 1], "exp", 4)
        first = first[:, :, 0] + first_came.astype(jnp.float32)
        second = second[:, 0] + second_came.astype(jnp.float32)
        first_came = exchanged(first[:, 1], "exp", 4)
        second_came = exchanged(second[:, 1], "exp", 2)
        first = first[:, 0] + first_came.astype(jnp.float32)
        second = second[:, 0] + second_came.astype(jnp.float32)
        mix = jnp.concatenate([first, second], axis=-1)
        mix = flipped_if(mix.reshape(2, 2, chunk_rows, model_width), segment // 2, 0)
        mix = mix[0] + exchanged(mix[1], "segment", 2).astype(jnp.float32)
        mix = flipped_if(mix, segment % 2, 0)
        mixes.append(mix[0] + exchanged(mix[1], "segment", 1).astype(jnp.float32))

    expert_mix = jnp.concatenate(mixes, axis=0).astype(jnp.bfloat16)
    combined = residual + expert_mix.astype(jnp.float32)
    normed_next = rms_norm(combined, latent_gain).astype(jnp.bfloat16)
    latents = jnp.dot(normed_next, kv_weight, preferred_element_type=jnp.float32).astype(
        jnp.bfloat16
    )
    gram_in, gram_hid = 0.0, 0.0
    for received, hidden, other_hidden in zip(all_received, all_hidden, all_other):
        own_columns = lax.dynamic_slice_in_dim(received, half_index * width_half, width_half, 1)
        gram_in = gram_in + lax.dot_general(
            own_columns, received, by_slots, preferred_element_type=jnp.float32
        )
        first_half = jnp.where(half_index == 0, hidden, other_hidden)
        second_half = jnp.where(half_index == 0, other_hidden, hidden)
        full_hidden = jnp.concatenate([first_half, second_half], axis=1)
        gram_hid = gram_hid + lax.dot_general(
            hidden, full_hidden, by_slots, preferred_element_type=jnp.float32
        )
    inverse_count = 2.0 / count
    return (
        expert_mix,
        latents,
        (gram_in * inverse_count)[None, None],
        (gram_hid * inverse_count)[None, None],
    )


def solution(mesh):
    return jax.shard_map(
        gather_body if mesh.shape["exp"] == 8 and mesh.shape["segment"] == 4 else dispatch_body,
        mesh=mesh,
        in_specs=(
            P(("segment", "exp"), None),
            P(),
            P(),
            P(("segment", "exp"), None),
            P("segment", "exp", None, None),
            P("segment", "exp", None, None),
            P("segment", "exp", None, None),
            P(),
            P(),
        ),
        out_specs=(
            P(("segment", "exp"), None),
            P(("segment", "exp"), None),
            P("segment", "exp", None, None),
            P("segment", "exp", None, None),
        ),
        check_vma=False,
    )
```

```python
import functools

import jax
import jax.numpy as jnp
from jax import lax
from jax.experimental import pallas as pl
from jax.experimental.pallas import tpu as pltpu
from jax.sharding import PartitionSpec as P

MB_TOK = 64


def swapped(value, axis, stride):
    mask = 2**stride
    pairs = [(source, source ^ mask) for source in range(lax.axis_size(axis))]
    return lax.ppermute(value, axis, pairs)


def rms_norm(values, gain):
    mean_square = jnp.mean(values * values, axis=-1, keepdims=True)
    return values * lax.rsqrt(mean_square + 1e-06) * gain


def dispatch_body(
    hidden_rows,
    norm_gain,
    router_weight,
    expert_ids,
    gate_weight,
    up_weight,
    down_weight,
    latent_gain,
    kv_weight,
):
    segments = lax.axis_size("segment")
    columns = lax.axis_size("exp")
    devices = segments * columns
    pair_count = segments // 2
    model_width = hidden_rows.shape[1]
    width_half = model_width // 2
    experts = router_weight.shape[1]
    top_count = expert_ids.shape[1]
    tok_rows = hidden_rows.shape[0]
    micro_rows = MB_TOK
    capacity = micro_rows * top_count * 5 // (4 * experts)
    half_index = lax.axis_index("segment") % 2
    w_gate = gate_weight[0, 0]
    w_up = up_weight[0, 0]
    w_down = down_weight[0, 0]
    half_units = w_gate.shape[0]
    slot_rows = devices * capacity
    own_rows = lax.dynamic_slice_in_dim(w_down, half_index * width_half, width_half, 1)
    sent_rows = lax.dynamic_slice_in_dim(w_down, (1 - half_index) * width_half, width_half, 1)
    other_rows = swapped(sent_rows, "segment", 0)
    down_block = jnp.where(
        half_index == 0,
        jnp.concatenate([own_rows, other_rows], axis=0),
        jnp.concatenate([other_rows, own_rows], axis=0),
    )
    residual = hidden_rows.astype(jnp.float32)
    normed = rms_norm(residual, norm_gain).astype(jnp.bfloat16)
    logits = jnp.dot(normed, router_weight, preferred_element_type=jnp.float32)
    expert_grid = jnp.arange(experts, dtype=jnp.int32)
    choose = expert_ids[:, :, None] == expert_grid[None, None, :]
    picked = jnp.sum(jnp.where(choose, logits[:, None, :], 0.0), axis=2)
    affinity = jax.nn.sigmoid(picked)
    gate_share = affinity / jnp.sum(affinity, axis=1, keepdims=True)
    gram_in = jnp.zeros((width_half, model_width), jnp.float32)
    gram_hid = jnp.zeros((half_units, 2 * half_units), jnp.float32)
    count_total = jnp.zeros((), jnp.float32)
    mix_blocks = []
    positions = jnp.arange(experts * capacity, dtype=jnp.int32)
    pair_rows = jnp.arange(micro_rows * top_count, dtype=jnp.int32)
    earlier = (pair_rows[:, None] > pair_rows[None, :]).astype(jnp.bfloat16)
    for step_index in range(tok_rows // micro_rows):
        low = step_index * micro_rows
        block_rows = normed[low : low + micro_rows]
        block_ids = expert_ids[low : low + micro_rows]
        block_gates = gate_share[low : low + micro_rows]
        flat_ids = block_ids.reshape(-1)
        onehot = (flat_ids[:, None] == expert_grid[None, :]).astype(jnp.int32)
        before = jnp.dot(
            earlier, onehot.astype(jnp.bfloat16), preferred_element_type=jnp.float32
        ).astype(jnp.int32)
        slot_rank = jnp.sum(before * onehot, axis=1)
        target = (flat_ids * capacity + slot_rank).reshape(micro_rows, top_count)
        picker = target[:, :, None] == positions[None, None, :]
        dispatch_table = jnp.any(picker, axis=1).astype(jnp.bfloat16)
        combine_table = jnp.sum(jnp.where(picker, block_gates[:, :, None], 0.0), axis=1)
        buffer = lax.dot_general(
            dispatch_table, block_rows, (((0,), (0,)), ((), ())), preferred_element_type=jnp.float32
        ).astype(jnp.bfloat16)
        sent_counts = jnp.sum(onehot, axis=0).astype(jnp.bfloat16)
        grid_rows = jnp.broadcast_to(
            buffer.reshape(pair_count, 1, columns, capacity, model_width),
            (pair_count, 2, columns, capacity, model_width),
        ).reshape(devices, capacity, model_width)
        grid_counts = jnp.broadcast_to(
            sent_counts.reshape(pair_count, 1, columns), (pair_count, 2, columns)
        ).reshape(devices, 1)
        arrived, arrived_counts = (
            lax.all_to_all(grid_rows, ("segment", "exp"), split_axis=0, concat_axis=0, tiled=True),
            lax.all_to_all(
                grid_counts, ("segment", "exp"), split_axis=0, concat_axis=0, tiled=True
            ),
        )
        received = arrived.reshape(slot_rows, model_width)
        count_total = count_total + jnp.sum(arrived_counts.astype(jnp.float32))
        gate_pre = lax.dot_general(
            w_gate, received, (((1,), (1,)), ((), ())), preferred_element_type=jnp.float32
        )
        up_pre = lax.dot_general(
            w_up, received, (((1,), (1,)), ((), ())), preferred_element_type=jnp.float32
        )
        hidden_t = (jax.nn.silu(gate_pre) * up_pre).astype(jnp.bfloat16)
        own_columns = lax.dynamic_slice_in_dim(received, half_index * width_half, width_half, 1)
        gram_in = gram_in + lax.dot_general(
            own_columns, received, (((0,), (0,)), ((), ())), preferred_element_type=jnp.float32
        )
        other_hidden = swapped(hidden_t, "segment", 0)
        first_half = jnp.where(half_index == 0, hidden_t, other_hidden)
        second_half = jnp.where(half_index == 0, other_hidden, hidden_t)
        full_hidden = jnp.concatenate([first_half, second_half], axis=0)
        gram_hid = gram_hid + lax.dot_general(
            hidden_t, full_hidden, (((1,), (1,)), ((), ())), preferred_element_type=jnp.float32
        )
        column_half = lax.dot_general(
            full_hidden, down_block, (((0,), (0,)), ((), ())), preferred_element_type=jnp.float32
        )
        returned = lax.all_to_all(
            column_half.reshape(devices, capacity, width_half),
            ("segment", "exp"),
            split_axis=0,
            concat_axis=0,
            tiled=True,
        )
        expert_rows = (
            returned.reshape(pair_count, 2, columns, capacity, width_half)
            .transpose(0, 2, 3, 1, 4)
            .reshape(experts * capacity, model_width)
        )
        mix_rows = jnp.dot(
            combine_table,
            expert_rows,
            precision=lax.Precision.HIGHEST,
            preferred_element_type=jnp.float32,
        )
        mix_blocks.append(mix_rows)
    expert_mix = jnp.concatenate(mix_blocks, axis=0).astype(jnp.bfloat16)
    combined = residual + expert_mix.astype(jnp.float32)
    normed_next = rms_norm(combined, latent_gain).astype(jnp.bfloat16)
    latents = jnp.dot(normed_next, kv_weight, preferred_element_type=jnp.float32).astype(
        jnp.bfloat16
    )
    inverse_count = 2.0 / count_total
    gram_input = (gram_in * inverse_count)[None, None]
    gram_hidden = (gram_hid * inverse_count)[None, None]
    return (expert_mix, latents, gram_input, gram_hidden)


CHUNKS = 4
PARTS = 3
PAD_ROWS = 16
MESH = pl.DeviceIdType.MESH
Z, X, Y, DIAG_A, DIAG_B, CORE = range(6)
UP, DOWN = 0, 9


def exchanged(value, axis, mask):
    pairs = [(source, source ^ mask) for source in range(lax.axis_size(axis))]
    return lax.ppermute(value.astype(jnp.bfloat16), axis, pairs)


def gate_table(normed, router_weight, expert_ids):
    experts = router_weight.shape[1]
    logits = jnp.dot(normed, router_weight, preferred_element_type=jnp.float32)
    grid = jnp.arange(experts, dtype=jnp.int32)
    choose = jnp.any(expert_ids[:, :, None] == grid[None, None, :], axis=1)
    affinity = jnp.where(choose, jax.nn.sigmoid(logits), 0.0)
    share = affinity / jnp.sum(affinity, axis=1, keepdims=True)
    return jnp.where(choose, share, -1.0)


def in_parts(table, width):
    parts, rest = [], table.reshape(-1)
    for _ in range(PARTS):
        part = lax.reduce_precision(rest, 8, 7)
        parts.append(part.astype(jnp.bfloat16))
        rest = rest - part
    flat = jnp.concatenate(parts)
    return jnp.pad(flat, (0, PAD_ROWS * width - flat.shape[0])).reshape(PAD_ROWS, width)


def gather_kernel(segments, in_ref, out_ref, send, recv, local):
    z, col = lax.axis_index("segment"), lax.axis_index("exp")
    c, x, y = col % 2, (col // 2) % 2, col // 4
    block = in_ref.shape[0]
    low = block // 32 * 16

    def place(yy, xx, cc):
        return yy * 4 + xx * 2 + cc

    x_side, y_side, c_side = place(y, 1 - x, c), place(1 - y, x, c), place(y, x, 1 - c)

    barrier = pltpu.get_barrier_semaphore()
    above, below = (z + 1) % segments, (z + segments - 1) % segments
    for peer in ((z, x_side), (z, y_side), (z, c_side), (above, col), (below, col)):
        pl.semaphore_signal(barrier, inc=1, device_id=peer, device_id_type=MESH)
    pl.semaphore_wait(barrier, 5)

    def copy(zz, source, kind, kind_there, target, start=0, size=block):
        ref = out_ref.at[pl.ds(pl.multiple_of((zz * 8 + source) * block + start, 16), size)]
        return pltpu.make_async_remote_copy(
            src_ref=ref,
            dst_ref=ref,
            send_sem=send.at[kind, zz],
            recv_sem=recv.at[kind_there, zz],
            device_id=target,
            device_id_type=MESH,
        )

    def up(zz):
        return copy(zz, col, UP, Z, (z + 1, col))

    def down(zz):
        return copy(zz, col, DOWN, Z, (z - 1, col))

    def to_x(zz):
        return copy(zz, col, X, X, (z, x_side))

    def to_y(zz):
        return copy(zz, col, Y, Y, (z, y_side))

    def diag_a(zz):
        return copy(zz, x_side, DIAG_A, DIAG_A, (z, y_side), 0, low)

    def diag_b(zz):
        return copy(zz, y_side, DIAG_B, DIAG_B, (z, x_side), low, block - low)

    def to_core(zz, yy, xx, number):
        return copy(zz, place(yy, xx, c), CORE + number, CORE + number, (z, c_side))

    def core_copies(zz):
        return [to_core(zz, y, x, 0), to_core(zz, y, 1 - x, 1), to_core(zz, 1 - y, x, 2)]

    diagonal = place(1 - y, 1 - x, c)

    def line(zz):
        @pl.when((zz <= z) & (z < segments - 1))
        def _():
            up(zz).start()

        @pl.when((zz >= z) & (z > 0))
        def _():
            down(zz).start()

        to_x(zz).start()
        to_y(zz).start()
        to_core(zz, y, x, 0).start()

    def arrived_line(zz):
        copy(zz, col, UP, Z, (z, c_side)).wait_recv()
        line(zz)

    def arrived_plane(zz):
        copy(zz, x_side, X, X, (z, x_side)).wait_recv()
        diag_a(zz).start()
        to_core(zz, y, 1 - x, 1).start()
        copy(zz, y_side, Y, Y, (z, y_side)).wait_recv()
        diag_b(zz).start()
        to_core(zz, 1 - y, x, 2).start()

    def arrived_diagonal(zz):
        copy(zz, diagonal, DIAG_A, DIAG_A, (z, y_side), 0, low).wait_recv()
        copy(zz, diagonal, DIAG_B, DIAG_B, (z, x_side), low, block - low).wait_recv()
        to_core(zz, 1 - y, 1 - x, 3).start()

    def at_distance(distance, step):
        if distance == 0:
            step(z)
            return
        for zz in (z - distance, z + distance):

            @pl.when((zz >= 0) & (zz < segments))
            def _():
                step(zz)

    own = pltpu.make_async_copy(
        in_ref, out_ref.at[pl.ds(pl.multiple_of((z * 8 + col) * block, 16), block)], local
    )
    own.start()
    own.wait()
    line(z)
    for distance in range(1, segments + 2):
        if distance < segments:
            at_distance(distance, arrived_line)
        if distance - 1 < segments:
            at_distance(distance - 1, arrived_plane)
        if distance >= 2:
            at_distance(distance - 2, arrived_diagonal)
    for zz in range(segments):
        for number, (yy, xx) in enumerate(((y, x), (y, 1 - x), (1 - y, x), (1 - y, 1 - x))):
            there = copy(
                zz, place(yy, xx, 1 - c), CORE + number, CORE + number, (z, c_side)
            )
            there.wait_recv()
            to_core(zz, yy, xx, number).wait_send()
        to_x(zz).wait_send()
        to_y(zz).wait_send()
        diag_a(zz).wait_send()
        diag_b(zz).wait_send()

        @pl.when((zz <= z) & (z < segments - 1))
        def _():
            up(zz).wait_send()

        @pl.when((zz >= z) & (z > 0))
        def _():
            down(zz).wait_send()


def gather_blocks(packed, segments, columns):
    block, width = packed.shape
    return pl.pallas_call(
        functools.partial(gather_kernel, segments),
        out_shape=jax.ShapeDtypeStruct((segments * columns * block, width), packed.dtype),
        in_specs=[pl.BlockSpec(memory_space=pl.ANY)],
        out_specs=pl.BlockSpec(memory_space=pl.ANY),
        scratch_shapes=[
            pltpu.SemaphoreType.DMA((10, segments)),
            pltpu.SemaphoreType.DMA((10, segments)),
            pltpu.SemaphoreType.DMA,
        ],
        compiler_params=pltpu.CompilerParams(collective_id=0, has_side_effects=True),
    )(packed)


def flipped_if(value, bit, dim):
    return jnp.where(bit == 1, jnp.flip(value, dim), value)


def gather_body(
    hidden_rows,
    norm_gain,
    router_weight,
    expert_ids,
    gate_weight,
    up_weight,
    down_weight,
    latent_gain,
    kv_weight,
):
    segment = lax.axis_index("segment")
    column = lax.axis_index("exp")
    columns = lax.axis_size("exp")
    segments = lax.axis_size("segment")
    half_index = segment % 2
    expert = (segment // 2) * columns + column
    core, along_x, along_y = column % 2, (column // 2) % 2, column // 4
    tok_rows, model_width = hidden_rows.shape
    width_half = model_width // 2
    experts = router_weight.shape[1]
    slot_rows = columns * tok_rows * expert_ids.shape[1] * 5 // (4 * experts)
    w_gate, w_up, w_down = gate_weight[0, 0], up_weight[0, 0], down_weight[0, 0]
    block = tok_rows + PAD_ROWS
    wide = columns * block

    residual = hidden_rows.astype(jnp.float32)
    normed = rms_norm(residual, norm_gain).astype(jnp.bfloat16)
    table = gate_table(normed, router_weight, expert_ids)
    packed = jnp.concatenate([normed, in_parts(table, model_width)], axis=0)
    gathered = gather_blocks(packed, segments, columns)
    tail = gathered.reshape(segments * columns, block, model_width)[:, tok_rows:]
    tail = tail.reshape(segments * columns, -1)[:, : PARTS * tok_rows * experts]
    tail = tail.reshape(-1, PARTS, tok_rows, experts).astype(jnp.float32)
    own = jnp.arange(experts, dtype=jnp.int32) == expert
    gates = jnp.sum(jnp.where(own, tail, 0.0), axis=(1, 3))
    gates = jnp.pad(gates, ((0, 0), (0, PAD_ROWS)), constant_values=-1.0).reshape(segments, wide)
    named = gates >= 0.0
    count = jnp.sum(named.astype(jnp.float32))
    where_at = jnp.arange(wide, dtype=jnp.int32)
    earlier = (where_at[:, None] < where_at[None, :]).astype(jnp.bfloat16)
    rank = jnp.dot(named.astype(jnp.bfloat16), earlier, preferred_element_type=jnp.float32)
    rank = jnp.where(named, rank.astype(jnp.int32), -1)
    slots = jnp.arange(slot_rows, dtype=jnp.int32)
    by_units = (((1,), (1,)), ((), ()))
    by_slots = (((0,), (0,)), ((), ()))
    picks = rank[:, None, :] == slots[None, :, None]
    slot_gates = jnp.sum(jnp.where(picks, gates[:, None, :], 0.0), axis=2)
    received = lax.dot_general(
        picks.astype(jnp.bfloat16),
        gathered.reshape(segments, wide, model_width),
        (((2,), (1,)), ((0,), (0,))),
        preferred_element_type=jnp.float32,
    ).astype(jnp.bfloat16)
    received = received.reshape(segments * slot_rows, model_width)
    gate_pre = lax.dot_general(received, w_gate, by_units, preferred_element_type=jnp.float32)
    up_pre = lax.dot_general(received, w_up, by_units, preferred_element_type=jnp.float32)
    hidden = (jax.nn.silu(gate_pre) * up_pre).astype(jnp.bfloat16)
    other_hidden = exchanged(hidden, "segment", 1)

    near = rank.reshape(segments, 2, 2, 2, block)[..., :tok_rows]
    near = flipped_if(flipped_if(flipped_if(near, core, 3), along_x, 2), along_y, 1)

    def scattered(places, out):
        hits = (places.reshape(segments, 1, -1) == slots[None, :, None]).astype(jnp.bfloat16)
        return lax.dot_general(
            hits, out, (((1,), (1,)), ((0,), (0,))), preferred_element_type=jnp.float32
        ).reshape(segments, 2, 2, tok_rows, -1)

    mixes = []
    width = model_width // CHUNKS
    for chunk in range(CHUNKS):
        own_down = w_down[:, chunk * width : (chunk + 1) * width]
        out = jnp.dot(hidden, own_down, preferred_element_type=jnp.float32)
        out = (out * slot_gates.reshape(-1, 1)).astype(jnp.bfloat16)
        out = out.reshape(segments, slot_rows, width)
        came = exchanged(scattered(near[:, :, :, 1], out), "exp", 1)
        mix = scattered(near[:, :, :, 0], out) + came.astype(jnp.float32)
        if chunk % 2 == 0:
            mix = mix[:, :, 0] + exchanged(mix[:, :, 1], "exp", 2).astype(jnp.float32)
            mix = mix[:, 0] + exchanged(mix[:, 1], "exp", 4).astype(jnp.float32)
        else:
            mix = mix[:, 0] + exchanged(mix[:, 1], "exp", 4).astype(jnp.float32)
            mix = mix[:, 0] + exchanged(mix[:, 1], "exp", 2).astype(jnp.float32)
        mix = flipped_if(mix.reshape(2, 2, tok_rows, width), segment // 2, 0)
        mix = mix[0] + exchanged(mix[1], "segment", 2).astype(jnp.float32)
        mix = flipped_if(mix, segment % 2, 0)
        mixes.append(mix[0] + exchanged(mix[1], "segment", 1).astype(jnp.float32))

    expert_mix = jnp.concatenate(mixes, axis=1).astype(jnp.bfloat16)
    combined = residual + expert_mix.astype(jnp.float32)
    normed_next = rms_norm(combined, latent_gain).astype(jnp.bfloat16)
    latents = jnp.dot(normed_next, kv_weight, preferred_element_type=jnp.float32).astype(
        jnp.bfloat16
    )
    own_columns = lax.dynamic_slice_in_dim(received, half_index * width_half, width_half, 1)
    gram_in = lax.dot_general(own_columns, received, by_slots, preferred_element_type=jnp.float32)
    first_half = jnp.where(half_index == 0, hidden, other_hidden)
    second_half = jnp.where(half_index == 0, other_hidden, hidden)
    full_hidden = jnp.concatenate([first_half, second_half], axis=1)
    gram_hid = lax.dot_general(hidden, full_hidden, by_slots, preferred_element_type=jnp.float32)
    inverse_count = 2.0 / count
    return (
        expert_mix,
        latents,
        (gram_in * inverse_count)[None, None],
        (gram_hid * inverse_count)[None, None],
    )


def solution(mesh):
    return jax.shard_map(
        gather_body if mesh.shape["exp"] == 8 and mesh.shape["segment"] == 4 else dispatch_body,
        mesh=mesh,
        in_specs=(
            P(("segment", "exp"), None),
            P(),
            P(),
            P(("segment", "exp"), None),
            P("segment", "exp", None, None),
            P("segment", "exp", None, None),
            P("segment", "exp", None, None),
            P(),
            P(),
        ),
        out_specs=(
            P(("segment", "exp"), None),
            P(("segment", "exp"), None),
            P("segment", "exp", None, None),
            P("segment", "exp", None, None),
        ),
        check_vma=False,
    )
```
